32 devices in a mesh: groups: 2 (over y), dom: 8 (over z, x), mp: 2 (over core).
Axes of the slice: x: 2, y: 2, z: 4, core: 2. Of those that a mesh axis runs over, the one named last changes fastest.
Arguments:
- node_latent: bfloat16 [1536, 512], P(('groups', 'dom')), parts along dimension 0, may hold values from -6 to 6
- edge_latent: bfloat16 [9216, 512], P(('groups', 'dom')), parts along dimension 0, may hold values from -6 to 6
- node_cot: bfloat16 [1536, 512], P(('groups', 'dom')), parts along dimension 0, may hold values from -6 to 6
- edge_cot: bfloat16 [9216, 512], P(('groups', 'dom')), parts along dimension 0, may hold values from -6 to 6
- edge_w1: bfloat16 [1536, 512], P(None, 'mp'), may hold values from -0.15625 to 0.15625
- edge_w2: bfloat16 [512, 512], P('mp'), may hold values from -0.25 to 0.25
- node_w1: bfloat16 [1024, 512], P(None, 'mp'), may hold values from -0.1875 to 0.1875
- node_w2: bfloat16 [512, 512], P('mp'), may hold values from -0.25 to 0.25
- send_rows: int32 [8, 6, 8], P('dom'), may hold values from 0 to 95
- edge_sender: int32 [4608], P('dom'), may hold values from 0 to 143, as said below
- edge_receiver: int32 [4608], P('dom'), may hold values from 0 to 95
- edge_count: int32 [8], P('dom'), may hold values from 288 to 576, as said below
Outputs:
- node_grad: bfloat16 [1536, 512], P(('groups', 'dom')), parts along dimension 0
- edge_grad: bfloat16 [9216, 512], P(('groups', 'dom')), parts along dimension 0
- edge_w1_grad: float32 [3072, 512], P(('groups', 'dom'), 'mp'), parts along dimension 0
- edge_w2_grad: float32 [1024, 512], P(('groups', 'mp'), 'dom'), parts along dimension 0
- node_w1_grad: float32 [2048, 512], P(('groups', 'dom'), 'mp'), parts along dimension 0
- node_w2_grad: float32 [1024, 512], P(('groups', 'mp'), 'dom'), parts along dimension 0
The draws below stay inside these ranges and needn't reach their ends.
There are 2 independent parts, one for each index of `groups`. The reference program is written for one: setup_inputs(seed, part) draws one part's arguments, and reference() takes and returns one part's arrays. A program takes and returns all parts, laid end to end along the dimension named above; an argument that names none is the same for every part. Nothing has to cross between parts.
Inputs may be any that keep to these rules, and one draw needn't show every extreme that they name: `edge_sender`: A code below 96 names a node of the edge's own partition; a code c of 96 or more names entry (c - 96) % 8 of the list that the edge's partition's neighbour number (c - 96) // 8 keeps for it. Among the first 48 slots of each block every code of 96 or more appears once. `edge_count`: some partition has all 576 slots live.
All inputs are finite; a program needn't handle non-finite values.
Results may differ from the reference program's by a relative error of at most 0.015.
Values may be sent and summed in bfloat16 or wider, within the bound.
A program may use at most 64 MiB of HBM per device.

```python
import jax
import jax.numpy as jnp
from jax import lax

D = 512
H = 512
NODE_DEV = 96
EDGE_CAP = 576
NEIGH = 6
SLOT = 8
NODES = 768
EDGES = 4608
N_DOM = 8
N_MP = 2


def draw_edge_sender(key, part):
    key = jax.random.fold_in(key, 11)
    remote_total = NEIGH * SLOT
    perm_key, pick_key, far_key, near_key = jax.random.split(key, 4)
    block_keys = jax.random.split(perm_key, N_DOM)
    listed = jax.vmap(lambda block_key: jax.random.permutation(block_key, remote_total))(block_keys)
    listed = listed.astype(jnp.int32) + NODE_DEV
    shape = (N_DOM, EDGE_CAP - remote_total)
    is_remote = jax.random.randint(pick_key, shape, 0, 5, dtype=jnp.int32) == 0
    far_codes = jax.random.randint(far_key, shape, NODE_DEV, NODE_DEV + remote_total, dtype=jnp.int32)
    near_codes = jax.random.randint(near_key, shape, 0, NODE_DEV, dtype=jnp.int32)
    others = jnp.where(is_remote, far_codes, near_codes)
    return jnp.concatenate([listed, others], axis=1).reshape(-1).astype(jnp.int32)


def draw_edge_count(key, part):
    key = jax.random.fold_in(key, 23)
    count_key, full_key = jax.random.split(key)
    lowest = max(NEIGH * SLOT, EDGE_CAP // 2)
    counts = jax.random.randint(count_key, (N_DOM,), lowest, EDGE_CAP + 1, dtype=jnp.int32)
    chosen = jax.random.randint(full_key, (), 0, N_DOM, dtype=jnp.int32)
    return jnp.where(jnp.arange(N_DOM, dtype=jnp.int32) == chosen, EDGE_CAP, counts).astype(jnp.int32)


def with_ends(entries, stream_key, low, largest):
    longest = entries.shape.index(max(entries.shape))
    spots = []
    for shift in (0, 1):
        where = [jax.random.randint(jax.random.fold_in(stream_key, axis), (), 0, length) for axis, length in enumerate(entries.shape)]
        where[longest] = (where[longest] + shift) % entries.shape[longest]
        spots.append(tuple(where))
    return entries.at[spots[0]].set(low).at[spots[1]].set(largest)


def block_levels(stream_key, dims, cuts, least, largest):
    def one(position, blocks):
        heights = jax.random.uniform(jax.random.fold_in(jax.random.fold_in(stream_key, 6), position), (blocks,), jnp.float32, least / len(cuts), largest / len(cuts))
        return jnp.repeat(jnp.exp(heights), dims[position] // blocks).reshape((-1,) + (1,) * (len(dims) - position - 1))

    level = one(*cuts[0])
    for cut in cuts[1:]:
        level = level * one(*cut)
    return level


def scatter_about(key, dims, deviation, most, cuts=(), kind=jnp.bfloat16):
    array = deviation * jax.random.normal(key, dims, jnp.float32)
    if cuts:
        array = array * block_levels(key, dims, cuts, -0.22, 0.18)
    return jnp.clip(array, -most, most).astype(kind)


def setup_inputs(seed: int = 0, part: int = 0) -> dict:
    seeds = jax.random.split(jax.random.key(seed), 13)
    part_keys = jax.random.split(jax.random.fold_in(seeds[12], part), 13)
    return {
        "node_latent": scatter_about(part_keys[0], (NODES, D), 1.0, 6.0, ((0, 8),)),
        "edge_latent": scatter_about(part_keys[1], (EDGES, D), 1.0, 6.0, ((0, 8),)),
        "node_cot": scatter_about(part_keys[2], (NODES, D), 1.0, 6.0, ((0, 8),)),
        "edge_cot": scatter_about(part_keys[3], (EDGES, D), 1.0, 6.0, ((0, 8),)),
        "edge_w1": scatter_about(seeds[4], (3 * D, H), (3 * D) ** -0.5, 0.15625, ((1, 2),)),
        "edge_w2": scatter_about(seeds[5], (H, D), H ** -0.5, 0.25, ((0, 2),)),
        "node_w1": scatter_about(seeds[6], (2 * D, H), (2 * D) ** -0.5, 0.1875, ((1, 2),)),
        "node_w2": scatter_about(seeds[7], (H, D), H ** -0.5, 0.25, ((0, 2),)),
        "send_rows": with_ends(jax.random.randint(seeds[8], (N_DOM, NEIGH, SLOT), 0, NODE_DEV), jax.random.fold_in(seeds[8], 1), 0, NODE_DEV - 1).astype(jnp.int32),
        "edge_sender": draw_edge_sender(jax.random.fold_in(seeds[12], 71), part),
        "edge_receiver": with_ends(jax.random.randint(seeds[10], (EDGES,), 0, NODE_DEV), jax.random.fold_in(seeds[10], 1), 0, NODE_DEV - 1).astype(jnp.int32),
        "edge_count": draw_edge_count(jax.random.fold_in(seeds[12], 71), part),
    }


EPS = 1e-05

def layer_norm(values):
    center = values - lax.optimization_barrier(jnp.mean(values, axis=-1, keepdims=True))
    inverse = lax.rsqrt(lax.optimization_barrier(jnp.mean(center * center, axis=-1, keepdims=True)) + EPS)
    return (center * inverse, inverse)

def norm_back(normed, inverse, upstream):
    first = lax.optimization_barrier(jnp.mean(upstream, axis=-1, keepdims=True))
    second = lax.optimization_barrier(jnp.mean(upstream * normed, axis=-1, keepdims=True))
    return inverse * (upstream - first - normed * second)

def silu_slope(values):
    sigma = jax.nn.sigmoid(values)
    return sigma * (1.0 + values * (1.0 - sigma))

def contract_rows(left, right):
    return lax.dot_general(left, right, (((0,), (0,)), ((), ())), preferred_element_type=jnp.float32)

def contract_cols(left, right):
    return lax.dot_general(left, right, (((1,), (1,)), ((), ())), preferred_element_type=jnp.float32)

def split_sum(upstream, weight):
    width = weight.shape[1] // N_MP
    total = jnp.zeros((upstream.shape[0], weight.shape[0]), jnp.float32)
    for half_index in range(N_MP):
        low = half_index * width
        piece = contract_cols(upstream[:, low:low + width], weight[:, low:low + width]).astype(jnp.bfloat16)
        total = total + piece.astype(jnp.float32)
    return total

def reference(node_latent, edge_latent, node_cot, edge_cot, edge_w1, edge_w2, node_w1, node_w2, send_rows, edge_sender, edge_receiver, edge_count):
    total_nodes = N_DOM * NODE_DEV
    half = NEIGH // 2
    positions = jnp.arange(N_DOM * EDGE_CAP, dtype=jnp.int32)
    block = positions // EDGE_CAP
    remote = jnp.maximum(edge_sender - NODE_DEV, 0)
    neighbour = remote // SLOT
    entry = remote % SLOT
    offset = jnp.where(neighbour < half, neighbour % half + 1, -(neighbour % half + 1)).astype(jnp.int32)
    source = ((block - offset) % N_DOM).astype(jnp.int32)
    listed = send_rows.reshape(-1)[(source * NEIGH + neighbour) * SLOT + entry]
    sender = jnp.where(edge_sender >= NODE_DEV, source * NODE_DEV + listed, block * NODE_DEV + edge_sender).astype(jnp.int32)
    receiver = (block * NODE_DEV + edge_receiver).astype(jnp.int32)
    live = (positions % EDGE_CAP < edge_count[block]).astype(jnp.float32)[:, None]
    edge_input = jnp.concatenate([edge_latent, node_latent[sender], node_latent[receiver]], axis=1)
    edge_pre = jnp.dot(edge_input, edge_w1, preferred_element_type=jnp.float32)
    edge_act = jax.nn.silu(edge_pre).astype(jnp.bfloat16)
    edge_out = jnp.dot(edge_act, edge_w2, preferred_element_type=jnp.float32)
    edge_normed, edge_inverse = layer_norm(edge_out)
    update_b = (live * edge_normed).astype(jnp.bfloat16)
    gathered = jax.ops.segment_sum(update_b.astype(jnp.float32), receiver, num_segments=total_nodes).astype(jnp.bfloat16)
    node_input = jnp.concatenate([node_latent, gathered], axis=1)
    node_pre = jnp.dot(node_input, node_w1, preferred_element_type=jnp.float32)
    node_act = jax.nn.silu(node_pre).astype(jnp.bfloat16)
    node_out = jnp.dot(node_act, node_w2, preferred_element_type=jnp.float32)
    node_normed, node_inverse = layer_norm(node_out)
    node_dout = norm_back(node_normed, node_inverse, node_cot.astype(jnp.float32)).astype(jnp.bfloat16)
    node_w2_grad = contract_rows(node_act, node_dout)
    node_dpre = (contract_cols(node_dout, node_w2) * silu_slope(node_pre)).astype(jnp.bfloat16)
    node_w1_grad = contract_rows(node_input, node_dpre)
    node_dinput = split_sum(node_dpre, node_w1)
    gathered_grad = node_dinput[:, D:].astype(jnp.bfloat16)
    edge_dup = live * (edge_cot.astype(jnp.float32) + gathered_grad[receiver].astype(jnp.float32))
    edge_dout = norm_back(edge_normed, edge_inverse, edge_dup).astype(jnp.bfloat16)
    edge_w2_grad = contract_rows(edge_act, edge_dout)
    edge_dpre = (contract_cols(edge_dout, edge_w2) * silu_slope(edge_pre)).astype(jnp.bfloat16)
    edge_w1_grad = contract_rows(edge_input, edge_dpre)
    edge_dinput = split_sum(edge_dpre, edge_w1)
    edge_grad = (live * (edge_cot.astype(jnp.float32) + edge_dinput[:, :D])).astype(jnp.bfloat16)
    sender_part = (live * edge_dinput[:, D:2 * D]).astype(jnp.bfloat16)
    receiver_part = (live * edge_dinput[:, 2 * D:]).astype(jnp.bfloat16)
    node_grad = node_cot.astype(jnp.float32) + node_dinput[:, :D]
    node_grad = node_grad + jax.ops.segment_sum(sender_part.astype(jnp.float32), sender, num_segments=total_nodes)
    node_grad = node_grad + jax.ops.segment_sum(receiver_part.astype(jnp.float32), receiver, num_segments=total_nodes)
    return (node_grad.astype(jnp.bfloat16), edge_grad, edge_w1_grad, edge_w2_grad, node_w1_grad, node_w2_grad)
```

```python
import functools

import jax
import jax.numpy as jnp
from jax import lax
from jax.experimental import pallas as pl
from jax.experimental.pallas import tpu as pltpu
from jax.sharding import PartitionSpec as P

EPS = 1e-05
BF = jnp.bfloat16
F32 = jnp.float32
MESH = pl.DeviceIdType.MESH
CHUNKS = 3


def dot(left, right, contract):
    return lax.dot_general(
        left, right, (((contract[0],), (contract[1],)), ((), ())), preferred_element_type=F32
    )


def nn(left, right):
    return dot(left, right, (1, 0))


def nt(left, right):
    return dot(left, right, (1, 1))


def tn(left, right):
    return dot(left, right, (0, 0))


def layer_norm(values):
    center = values - jnp.mean(values, axis=-1, keepdims=True)
    inverse = lax.rsqrt(jnp.mean(center * center, axis=-1, keepdims=True) + EPS)
    return (center * inverse, inverse)


def norm_back(normed, inverse, upstream):
    first = jnp.mean(upstream, axis=-1, keepdims=True)
    second = jnp.mean(upstream * normed, axis=-1, keepdims=True)
    return inverse * (upstream - first - normed * second)


def silu_and_slope(values):
    sigma = jax.nn.sigmoid(values)
    return values * sigma, sigma * (1.0 + values * (1.0 - sigma))


def offset_of(index, half):
    return (index % half + 1) * (1 if index < half else -1)


def kernel(
    dims,
    node_ref,
    edge_ref,
    ncot_ref,
    ecot_ref,
    w1_ref,
    w2_ref,
    nw1_ref,
    nw2_ref,
    codes_ref,
    ngrad_ref,
    egrad_ref,
    ew1_out,
    ew2_out,
    nw1_out,
    nw2_out,
    pick,
    pick_t,
    live,
    halo_out,
    halo_in,
    sources,
    table,
    pre,
    act,
    slope,
    mine,
    theirs,
    normed,
    inverse,
    upd,
    nmine,
    ntheirs,
    gmine,
    gtheirs,
    dout,
    dpre,
    dmine,
    dtheirs,
    back_out,
    back_in,
    fmine,
    ftheirs,
    nbuf,
    np1,
    nsum,
    np2,
    ebuf,
    ep1,
    esum,
    ep2,
    halo_s,
    halo_r,
    back_s,
    back_r,
    mp_s,
    mp_r,
    n1_s,
    n1_r,
    n2_s,
    n2_r,
    e1_s,
    e1_r,
    e2_s,
    e2_r,
):
    count, neigh, slots, scatter = dims
    me = lax.axis_index("dom")
    core = lax.axis_index("mp")
    other = {"mp": 1 - core}
    nodes, width = node_ref.shape
    edges = edge_ref.shape[0]
    hidden = w2_ref.shape[0]
    listed = neigh * slots
    codes = nodes + listed
    rows = edges // CHUNKS
    half = neigh // 2

    def at(shift):
        return {"dom": lax.rem(me + shift + count, count)}

    def remote(src, dst, send, recv, device):
        return pltpu.make_async_remote_copy(
            src_ref=src,
            dst_ref=dst,
            send_sem=send,
            recv_sem=recv,
            device_id=device,
            device_id_type=MESH,
        )

    barrier = pltpu.get_barrier_semaphore()
    shifts = sorted({offset_of(k, half) % count for k in range(neigh)})
    shifts = sorted(set(shifts) | {(-s) % count for s in shifts})
    if scatter:
        shifts = list(range(1, count))
    for shift in shifts:
        pl.semaphore_signal(barrier, inc=1, device_id=at(shift), device_id_type=MESH)
    pl.semaphore_signal(barrier, inc=1, device_id=other, device_id_type=MESH)

    spread = codes_ref[...]
    place = lax.broadcasted_iota(jnp.int32, (pick.shape[0], spread.shape[1]), 0)
    hit = (place == spread[0:1, :]) | (place == spread[1:2, :])
    pick_f = jnp.where(hit, 1.0, 0.0).astype(F32)
    pick[...] = pick_f[:, :edges].astype(BF)
    send_place = lax.broadcasted_iota(jnp.int32, (nodes, listed), 0)
    lists = jnp.where(send_place == spread[2:3, :listed], 1.0, 0.0).astype(F32).astype(BF)
    node = node_ref[...]
    halo_out[...] = tn(lists, node)

    pl.semaphore_wait(barrier, len(shifts) + 1)
    halo = []
    for k in range(neigh):
        block = pl.ds(k * slots, slots)
        copy = remote(
            halo_out.at[block], halo_in.at[block], halo_s.at[k], halo_r.at[k],
            at(offset_of(k, half)),
        )
        copy.start()
        halo.append(copy)

    picked = jnp.transpose(pick_f)[:edges]
    pick_t[...] = picked.astype(BF)
    live[...] = jnp.max(picked, axis=1, keepdims=True)
    pre[...] = nn(edge_ref[...], w1_ref[0:width])
    table[0:nodes] = nn(node, w1_ref[width : 2 * width]).astype(BF)
    table[codes : codes + nodes] = nn(node, w1_ref[2 * width : 3 * width]).astype(BF)
    if pick.shape[0] > codes + nodes:
        table[codes + nodes :] = jnp.zeros((pick.shape[0] - codes - nodes, hidden), BF)
    sources[0:nodes] = node
    for copy in halo:
        copy.wait_recv()
    arrived = halo_in[...].astype(BF)
    sources[nodes:codes] = arrived
    table[nodes:codes] = nn(arrived, w1_ref[width : 2 * width]).astype(BF)

    trades = []
    for c in range(CHUNKS):
        r = pl.ds(c * rows, rows)
        values = pre[r] + nn(pick_t[r], table[...])
        a, s = silu_and_slope(values)
        a = a.astype(BF)
        act[r] = a
        slope[r] = s
        mine[r] = nn(a, w2_ref[...]).astype(BF)
        copy = remote(mine.at[r], theirs.at[r], mp_s.at[c], mp_r.at[c], other)
        copy.start()
        trades.append(copy)
    node_first = nn(node, nw1_ref[0:width])
    for c in range(CHUNKS):
        r = pl.ds(c * rows, rows)
        trades[c].wait_recv()
        n, i = layer_norm(mine[r].astype(F32) + theirs[r].astype(F32))
        normed[r] = n
        inverse[r] = i
        upd[r] = n.astype(BF)
    gathered = nn(pick[codes : codes + nodes], upd[...]).astype(BF)

    node_act, node_slope = silu_and_slope(node_first + nn(gathered, nw1_ref[width : 2 * width]))
    node_act = node_act.astype(BF)
    nmine[...] = nn(node_act, nw2_ref[...]).astype(BF)
    trade = remote(nmine, ntheirs, mp_s.at[CHUNKS], mp_r.at[CHUNKS], other)
    trade.start()
    trades.append(trade)
    trade.wait_recv()
    n, i = layer_norm(nmine[...].astype(F32) + ntheirs[...].astype(F32))
    node_dout = norm_back(n, i, ncot_ref[...].astype(F32)).astype(BF)
    node_dpre = (nt(node_dout, nw2_ref[...]) * node_slope).astype(BF)
    gmine[...] = nt(node_dpre, nw1_ref[width : 2 * width]).astype(BF)
    trade = remote(gmine, gtheirs, mp_s.at[CHUNKS + 1], mp_r.at[CHUNKS + 1], other)
    trade.start()
    trades.append(trade)

    pairs = count // 2
    x = lax.rem(me, 2)
    z = lax.div(me, 2)
    order = list(range(1, pairs)) + [0]

    def turn(k):
        return lax.rem(z + k, pairs)

    def place_slices(buf, first, second):
        a = first.shape[0] // count
        b = second.shape[0] // count
        for j in range(count):
            buf[j % 2, j // 2, 0:a] = first[j * a : (j + 1) * a].astype(BF)
            buf[j % 2, j // 2, a : a + b] = second[j * b : (j + 1) * b].astype(BF)

    def first_phase(buf, land, send, recv):
        copies = {}
        for k in order:
            copies[k] = remote(
                buf.at[1 - x, turn(k)], land.at[turn(k)], send.at[k], recv.at[k],
                {"dom": me + 1 - 2 * x},
            )
            copies[k].start()
        return copies

    def second_phase(copies, buf, land, summed, land2, send, recv):
        later = []
        for k in range(1, pairs):
            copies[k].wait_recv()
            total = buf[x, turn(k)].astype(F32) + land[turn(k)].astype(F32)
            summed[k - 1] = total.astype(BF)
            copy = remote(
                summed.at[k - 1], land2.at[k - 1], send.at[k - 1], recv.at[k - 1],
                {"dom": turn(k) * 2 + x},
            )
            copy.start()
            later.append(copy)
        return later

    def finish(copies, later, buf, land, land2, out_a, out_b):
        copies[0].wait_recv()
        total = buf[x, z].astype(F32) + land[z].astype(F32)
        for k in range(1, pairs):
            later[k - 1].wait_recv()
            total = total + land2[k - 1].astype(F32)
        a = out_a.shape[0]
        out_a[...] = total[:a]
        out_b[...] = total[a:]

    node_w1_grad = jnp.concatenate([tn(node, node_dpre), tn(gathered, node_dpre)], axis=0)
    node_w2_grad = tn(node_dout, node_act)
    if scatter:
        place_slices(nbuf, node_w1_grad, node_w2_grad)
        n_first = first_phase(nbuf, np1, n1_s, n1_r)
    else:
        nw1_out[...] = node_w1_grad
        nw2_out[...] = node_w2_grad
    node_own = nt(node_dpre, nw1_ref[0:width])

    trade.wait_recv()
    gathered_grad = (gmine[...].astype(F32) + gtheirs[...].astype(F32)).astype(BF)
    for c in range(CHUNKS):
        r = pl.ds(c * rows, rows)
        upstream = live[r] * ecot_ref[r].astype(F32) + nn(
            pick_t[r, codes : codes + nodes], gathered_grad
        )
        d = norm_back(normed[r], inverse[r], upstream).astype(BF)
        dout[r] = d
        dpre[r] = (nt(d, w2_ref[...]) * slope[r]).astype(BF)
    if scatter:
        n_later = second_phase(n_first, nbuf, np1, nsum, np2, n2_s, n2_r)
    sums = nn(pick[...], dpre[...]).astype(BF)
    by_code = sums[0:codes]
    by_node = sums[codes : codes + nodes]
    edge_w1_grad = jnp.concatenate(
        [tn(edge_ref[...], dpre[...]), tn(sources[...], by_code), tn(node, by_node)], axis=0
    )
    edge_w2_grad = tn(dout[...], act[...])
    if scatter:
        place_slices(ebuf, edge_w1_grad, edge_w2_grad)
        e_first = first_phase(ebuf, ep1, e1_s, e1_r)
    else:
        ew1_out[...] = edge_w1_grad
        ew2_out[...] = edge_w2_grad

    per_code = nt(by_code, w1_ref[width : 2 * width])
    back_out[...] = per_code[nodes:codes]
    backs = []
    for k in range(neigh):
        block = pl.ds(k * slots, slots)
        copy = remote(
            back_out.at[block], back_in.at[block], back_s.at[k], back_r.at[k],
            at(-offset_of(k, half)),
        )
        copy.start()
        backs.append(copy)
    edge_trades = []
    for c in range(CHUNKS):
        r = pl.ds(c * rows, rows)
        dmine[r] = nt(dpre[r], w1_ref[0:width]).astype(BF)
        s = CHUNKS + 2 + c
        copy = remote(dmine.at[r], dtheirs.at[r], mp_s.at[s], mp_r.at[s], other)
        copy.start()
        edge_trades.append(copy)
    node_own = node_own + per_code[0:nodes] + nt(by_node, w1_ref[2 * width : 3 * width])
    if scatter:
        e_later = second_phase(e_first, ebuf, ep1, esum, ep2, e2_s, e2_r)
    for copy in backs:
        copy.wait_recv()
    fmine[...] = node_own + nn(lists, back_in[...].astype(BF))
    last = 2 * CHUNKS + 2
    final = remote(fmine, ftheirs, mp_s.at[last], mp_r.at[last], other)
    final.start()
    for c in range(CHUNKS):
        r = pl.ds(c * rows, rows)
        edge_trades[c].wait_recv()
        total = dmine[r].astype(F32) + dtheirs[r].astype(F32)
        egrad_ref[r] = (live[r] * (ecot_ref[r].astype(F32) + total)).astype(BF)
    final.wait_recv()
    ngrad_ref[...] = (ncot_ref[...].astype(F32) + fmine[...] + ftheirs[...]).astype(BF)
    if scatter:
        finish(n_first, n_later, nbuf, np1, np2, nw1_out, nw2_out)
        finish(e_first, e_later, ebuf, ep1, ep2, ew1_out, ew2_out)
        for copy in list(n_first.values()) + n_later + list(e_first.values()) + e_later:
            copy.wait_send()
    for copy in halo + trades + backs + edge_trades + [final]:
        copy.wait_send()


def local(
    count,
    node_latent,
    edge_latent,
    node_cot,
    edge_cot,
    edge_w1,
    edge_w2,
    node_w1,
    node_w2,
    send_rows,
    edge_sender,
    edge_receiver,
    edge_count,
):
    nodes, width = node_latent.shape
    edges = edge_latent.shape[0]
    hidden = edge_w1.shape[1]
    neigh, slots = send_rows.shape[1:]
    listed = neigh * slots
    codes = nodes + listed
    total = -(-(codes + nodes) // 128) * 128
    padded = -(-edges // 128) * 128
    live = jnp.arange(edges, dtype=jnp.int32) < edge_count[0]
    fill = padded - edges
    spread = jnp.stack(
        [
            jnp.pad(jnp.where(live, edge_sender, -1), (0, fill), constant_values=-1),
            jnp.pad(jnp.where(live, edge_receiver + codes, -1), (0, fill), constant_values=-1),
            jnp.pad(send_rows.reshape(-1), (0, padded - listed), constant_values=-1),
        ]
    )
    spread = jnp.pad(spread, ((0, 5), (0, 0)), constant_values=-1)
    w1_rows, nw1_rows = edge_w1.shape[0], node_w1.shape[0]
    scatter = (
        count % 2 == 0
        and w1_rows % (16 * count) == 0
        and nw1_rows % (16 * count) == 0
        and width % (16 * count) == 0
    )
    parts = count if scatter else 1
    pairs = max(count // 2, 2) if scatter else 2
    n_rows = (nw1_rows + width) // parts if scatter else 16
    e_rows = (w1_rows + width) // parts if scatter else 16
    vmem = pltpu.VMEM
    dma = pltpu.SemaphoreType.DMA
    scratch = [
        vmem((total, edges), BF),
        vmem((edges, total), BF),
        vmem((edges, 1), F32),
        vmem((listed, width), F32),
        vmem((listed, width), F32),
        vmem((codes, width), BF),
        vmem((total, hidden), BF),
        vmem((edges, hidden), F32),
        vmem((edges, hidden), BF),
        vmem((edges, hidden), F32),
        vmem((edges, width), BF),
        vmem((edges, width), BF),
        vmem((edges, width), F32),
        vmem((edges, 1), F32),
        vmem((edges, width), BF),
        vmem((nodes, width), BF),
        vmem((nodes, width), BF),
        vmem((nodes, width), BF),
        vmem((nodes, width), BF),
        vmem((edges, width), BF),
        vmem((edges, hidden), BF),
        vmem((edges, width), BF),
        vmem((edges, width), BF),
        vmem((listed, width), F32),
        vmem((listed, width), F32),
        vmem((nodes, width), F32),
        vmem((nodes, width), F32),
        vmem((2, pairs, n_rows, hidden), BF),
        vmem((pairs, n_rows, hidden), BF),
        vmem((pairs - 1, n_rows, hidden), BF),
        vmem((pairs - 1, n_rows, hidden), BF),
        vmem((2, pairs, e_rows, hidden), BF),
        vmem((pairs, e_rows, hidden), BF),
        vmem((pairs - 1, e_rows, hidden), BF),
        vmem((pairs - 1, e_rows, hidden), BF),
        dma((neigh,)),
        dma((neigh,)),
        dma((neigh,)),
        dma((neigh,)),
        dma((2 * CHUNKS + 3,)),
        dma((2 * CHUNKS + 3,)),
        dma((pairs,)),
        dma((pairs,)),
        dma((pairs - 1,)),
        dma((pairs - 1,)),
        dma((pairs,)),
        dma((pairs,)),
        dma((pairs - 1,)),
        dma((pairs - 1,)),
    ]
    shape = jax.ShapeDtypeStruct
    node_grad, edge_grad, ew1, ew2, nw1, nw2 = pl.pallas_call(
        functools.partial(kernel, (count, neigh, slots, scatter)),
        out_shape=(
            shape((nodes, width), BF),
            shape((edges, width), BF),
            shape((w1_rows // parts, hidden), F32),
            shape((width // parts, hidden), F32),
            shape((nw1_rows // parts, hidden), F32),
            shape((width // parts, hidden), F32),
        ),
        in_specs=[pl.BlockSpec(memory_space=pltpu.VMEM)] * 9,
        out_specs=[pl.BlockSpec(memory_space=pltpu.VMEM)] * 6,
        scratch_shapes=scratch,
        compiler_params=pltpu.CompilerParams(
            collective_id=0, has_side_effects=True, vmem_limit_bytes=50 * 1024 * 1024
        ),
    )(
        node_latent, edge_latent, node_cot, edge_cot, edge_w1, edge_w2, node_w1, node_w2, spread
    )
    ew2, nw2 = ew2.T, nw2.T
    if not scatter:
        ew1, nw1 = (
            lax.psum_scatter(g, "dom", scatter_dimension=0, tiled=True) for g in (ew1, nw1)
        )
        ew2, nw2 = (
            lax.psum_scatter(g, "dom", scatter_dimension=1, tiled=True) for g in (ew2, nw2)
        )
    return node_grad, edge_grad, ew1, ew2, nw1, nw2


def solution(mesh):
    placed = (
        P(("groups", "dom"), None),
        P(("groups", "dom"), None),
        P(("groups", "dom"), None),
        P(("groups", "dom"), None),
        P(None, "mp"),
        P("mp", None),
        P(None, "mp"),
        P("mp", None),
        P("dom", None, None),
        P("dom"),
        P("dom"),
        P("dom"),
    )
    return jax.shard_map(
        functools.partial(local, mesh.shape["dom"]),
        mesh=mesh,
        in_specs=placed,
        out_specs=(
            P(("groups", "dom"), None),
            P(("groups", "dom"), None),
            P(("groups", "dom"), "mp"),
            P(("groups", "mp"), "dom"),
            P(("groups", "dom"), "mp"),
            P(("groups", "mp"), "dom"),
        ),
        check_vma=False,
    )
```

```python
import functools

import jax
import jax.numpy as jnp
from jax import lax
from jax.experimental import pallas as pl
from jax.experimental.pallas import tpu as pltpu
from jax.sharding import PartitionSpec as P

EPS = 1e-05
BF = jnp.bfloat16
F32 = jnp.float32
MESH = pl.DeviceIdType.MESH
CHUNKS = 3
VMEM_LIMIT = 62 * 1024 * 1024


def dot(left, right, contract):
    return lax.dot_general(
        left, right, (((contract[0],), (contract[1],)), ((), ())), preferred_element_type=F32
    )


def nn(left, right):
    return dot(left, right, (1, 0))


def nt(left, right):
    return dot(left, right, (1, 1))


def tn(left, right):
    return dot(left, right, (0, 0))


def layer_norm(values):
    center = values - jnp.mean(values, axis=-1, keepdims=True)
    inverse = lax.rsqrt(jnp.mean(center * center, axis=-1, keepdims=True) + EPS)
    return (center * inverse, inverse)


def norm_back(normed, inverse, upstream):
    first = jnp.mean(upstream, axis=-1, keepdims=True)
    second = jnp.mean(upstream * normed, axis=-1, keepdims=True)
    return inverse * (upstream - first - normed * second)


def silu_and_slope(values):
    sigma = jax.nn.sigmoid(values)
    return values * sigma, sigma * (1.0 + values * (1.0 - sigma))


def offset_of(index, half):
    return (index % half + 1) * (1 if index < half else -1)


def kernel(
    dims,
    node_hbm,
    edge_hbm,
    ncot_hbm,
    ecot_hbm,
    w1_hbm,
    w2_hbm,
    nw1_hbm,
    nw2_hbm,
    send_hbm,
    sender_hbm,
    receiver_hbm,
    count_ref,
    ngrad_hbm,
    egrad_hbm,
    ew1_hbm,
    ew2_hbm,
    nw1_grad_hbm,
    nw2_grad_hbm,
    ngrad_ref,
    egrad_ref,
    ew1_out,
    ew2_out,
    nw1_out,
    nw2_out,
    node_ref,
    edge_ref,
    ncot_ref,
    ecot_ref,
    w1_ref,
    w2_ref,
    nw1_ref,
    nw2_ref,
    send_ref,
    sender_ref,
    receiver_ref,
    lists_ref,
    pick,
    pick_t,
    live,
    halo_out,
    halo_in,
    sources,
    table,
    pre,
    act,
    slope,
    mine,
    theirs,
    normed,
    inverse,
    upd,
    nmine,
    ntheirs,
    gmine,
    gtheirs,
    dout,
    dpre,
    dmine,
    dtheirs,
    back_out,
    back_in,
    fmine,
    ftheirs,
    nbuf,
    np1,
    nsum,
    np2,
    ebuf,
    ep1,
    esum,
    ep2,
    halo_s,
    halo_r,
    back_s,
    back_r,
    mp_s,
    mp_r,
    n1_s,
    n1_r,
    n2_s,
    n2_r,
    e1_s,
    e1_r,
    e2_s,
    e2_r,
    load_s,
):
    count, neigh, slots, scatter = dims
    me = lax.axis_index("dom")
    core = lax.axis_index("mp")
    other = {"mp": 1 - core}
    nodes, width = node_ref.shape
    edges = edge_ref.shape[0]
    hidden = w2_ref.shape[0]
    listed = neigh * slots
    codes = nodes + listed
    rows = edges // CHUNKS
    half = neigh // 2

    def at(shift):
        return {"dom": lax.rem(me + shift + count, count)}

    def remote(src, dst, send, recv, device):
        return pltpu.make_async_remote_copy(
            src_ref=src,
            dst_ref=dst,
            send_sem=send,
            recv_sem=recv,
            device_id=device,
            device_id_type=MESH,
        )

    def load(index, src, dst):
        copy = pltpu.make_async_copy(src, dst, load_s.at[index])
        copy.start()
        return copy

    loads = [
        load(0, send_hbm, send_ref),
        load(1, node_hbm, node_ref),
        load(2, sender_hbm, sender_ref),
        load(3, receiver_hbm, receiver_ref),
        load(4, edge_hbm, edge_ref),
        load(5, w1_hbm, w1_ref),
        load(6, w2_hbm, w2_ref),
        load(7, nw1_hbm, nw1_ref),
        load(8, nw2_hbm, nw2_ref),
        load(9, ncot_hbm, ncot_ref),
        load(10, ecot_hbm, ecot_ref),
    ]
    barrier = pltpu.get_barrier_semaphore()
    shifts = sorted({offset_of(k, half) % count for k in range(neigh)})
    shifts = sorted(set(shifts) | {(-s) % count for s in shifts})
    if scatter:
        shifts = list(range(1, count))
    for shift in shifts:
        pl.semaphore_signal(barrier, inc=1, device_id=at(shift), device_id_type=MESH)
    pl.semaphore_signal(barrier, inc=1, device_id=other, device_id_type=MESH)

    send_place = lax.broadcasted_iota(jnp.int32, (nodes, slots), 0)
    loads[0].wait()
    for k in range(neigh):
        hit = send_place == send_ref[k]
        lists_ref[:, k * slots : (k + 1) * slots] = jnp.where(hit, 1.0, 0.0).astype(F32)
    lists = lists_ref[...].astype(BF)
    loads[1].wait()
    node = node_ref[...]
    halo_out[...] = tn(lists, node)
    loads[2].wait()
    loads[3].wait()
    place = lax.broadcasted_iota(jnp.int32, pick.shape, 0)
    alive = lax.broadcasted_iota(jnp.int32, pick.shape, 1) < count_ref[0]
    hit = (place == sender_ref[...][None, :]) | (place == receiver_ref[...][None, :] + codes)
    pick_f = jnp.where(hit & alive, 1.0, 0.0).astype(F32)
    pick[...] = pick_f.astype(BF)

    pl.semaphore_wait(barrier, len(shifts) + 1)
    halo = []
    for k in range(neigh):
        block = pl.ds(k * slots, slots)
        copy = remote(
            halo_out.at[block], halo_in.at[block], halo_s.at[k], halo_r.at[k],
            at(offset_of(k, half)),
        )
        copy.start()
        halo.append(copy)

    picked = jnp.transpose(pick_f)
    pick_t[...] = picked.astype(BF)
    live[...] = jnp.max(picked, axis=1, keepdims=True)
    loads[4].wait()
    loads[5].wait()
    pre[...] = nn(edge_ref[...], w1_ref[0:width])
    table[0:nodes] = nn(node, w1_ref[width : 2 * width]).astype(BF)
    table[codes : codes + nodes] = nn(node, w1_ref[2 * width : 3 * width]).astype(BF)
    if pick.shape[0] > codes + nodes:
        table[codes + nodes :] = jnp.zeros((pick.shape[0] - codes - nodes, hidden), BF)
    sources[0:nodes] = node
    for copy in halo:
        copy.wait_recv()
    arrived = halo_in[...].astype(BF)
    sources[nodes:codes] = arrived
    table[nodes:codes] = nn(arrived, w1_ref[width : 2 * width]).astype(BF)

    loads[6].wait()
    trades = []
    for c in range(CHUNKS):
        r = pl.ds(c * rows, rows)
        values = pre[r] + nn(pick_t[r], table[...])
        a, s = silu_and_slope(values)
        a = a.astype(BF)
        act[r] = a
        slope[r] = s
        mine[r] = nn(a, w2_ref[...]).astype(BF)
        copy = remote(mine.at[r], theirs.at[r], mp_s.at[c], mp_r.at[c], other)
        copy.start()
        trades.append(copy)
    for copy in loads[7:]:
        copy.wait()
    node_first = nn(node, nw1_ref[0:width])
    for c in range(CHUNKS):
        r = pl.ds(c * rows, rows)
        trades[c].wait_recv()
        n, i = layer_norm(mine[r].astype(F32) + theirs[r].astype(F32))
        normed[r] = n
        inverse[r] = i
        upd[r] = n.astype(BF)
    gathered = nn(pick[codes : codes + nodes], upd[...]).astype(BF)

    node_act, node_slope = silu_and_slope(node_first + nn(gathered, nw1_ref[width : 2 * width]))
    node_act = node_act.astype(BF)
    nmine[...] = nn(node_act, nw2_ref[...]).astype(BF)
    trade = remote(nmine, ntheirs, mp_s.at[CHUNKS], mp_r.at[CHUNKS], other)
    trade.start()
    trades.append(trade)
    trade.wait_recv()
    n, i = layer_norm(nmine[...].astype(F32) + ntheirs[...].astype(F32))
    node_dout = norm_back(n, i, ncot_ref[...].astype(F32)).astype(BF)
    node_dpre = (nt(node_dout, nw2_ref[...]) * node_slope).astype(BF)
    gmine[...] = nt(node_dpre, nw1_ref[width : 2 * width]).astype(BF)
    trade = remote(gmine, gtheirs, mp_s.at[CHUNKS + 1], mp_r.at[CHUNKS + 1], other)
    trade.start()
    trades.append(trade)

    x = lax.rem(me, 2)
    z = lax.div(me, 2)
    near = z + 1 - 2 * lax.rem(z, 2)
    turns = [lax.rem(near + 2, 4), near, lax.rem(z + 2, 4), z]

    def place_slices(buf, first, second):
        a = first.shape[0] // count
        b = second.shape[0] // count
        for j in range(count):
            buf[j % 2, j // 2, 0:a] = first[j * a : (j + 1) * a].astype(BF)
            buf[j % 2, j // 2, a : a + b] = second[j * b : (j + 1) * b].astype(BF)

    def across_x(buf, land, send, recv):
        copies = []
        for k in range(4):
            copy = remote(
                buf.at[1 - x, turns[k]], land.at[k], send.at[k], recv.at[k],
                {"dom": me + 1 - 2 * x},
            )
            copy.start()
            copies.append(copy)
        return copies

    def along_z(k, copies, buf, land, summed, land2, send, recv):
        copies[k].wait_recv()
        total = buf[x, turns[k]].astype(F32) + land[k].astype(F32)
        if k == 2:
            copies[4].wait_recv()
            total = total + land2[0].astype(F32)
        summed[k] = total.astype(BF)
        copy = remote(
            summed.at[k], land2.at[k], send.at[k], recv.at[k],
            {"dom": (near if k < 2 else turns[2]) * 2 + x},
        )
        copy.start()
        copies.append(copy)

    def finish(copies, buf, land, summed, land2, out_a, out_b):
        copies[3].wait_recv()
        copies[5].wait_recv()
        total = buf[x, z].astype(F32) + land[3].astype(F32) + land2[1].astype(F32)
        copies[6].wait_recv()
        total = total + land2[2].astype(F32)
        a = out_a.shape[0]
        out_a[...] = total[:a]
        out_b[...] = total[a:]

    node_w1_grad = jnp.concatenate([tn(node, node_dpre), tn(gathered, node_dpre)], axis=0)
    node_w2_grad = tn(node_dout, node_act)
    if scatter:
        place_slices(nbuf, node_w1_grad, node_w2_grad)
        n_copies = across_x(nbuf, np1, n1_s, n1_r)
        n_rest = (n_copies, nbuf, np1, nsum, np2)
    else:
        nw1_out[...] = node_w1_grad
        nw2_out[...] = node_w2_grad
    node_own = nt(node_dpre, nw1_ref[0:width])

    trade.wait_recv()
    gathered_grad = (gmine[...].astype(F32) + gtheirs[...].astype(F32)).astype(BF)
    for c in range(CHUNKS):
        r = pl.ds(c * rows, rows)
        upstream = live[r] * ecot_ref[r].astype(F32) + nn(
            pick_t[r, codes : codes + nodes], gathered_grad
        )
        d = norm_back(normed[r], inverse[r], upstream).astype(BF)
        dout[r] = d
        dpre[r] = (nt(d, w2_ref[...]) * slope[r]).astype(BF)
        if scatter and c > 0:
            along_z(c - 1, *n_rest, n2_s, n2_r)
    sums = nn(pick[...], dpre[...]).astype(BF)
    by_code = sums[0:codes]
    by_node = sums[codes : codes + nodes]
    edge_w1_grad = jnp.concatenate(
        [tn(edge_ref[...], dpre[...]), tn(sources[...], by_code), tn(node, by_node)], axis=0
    )
    edge_w2_grad = tn(dout[...], act[...])
    if scatter:
        place_slices(ebuf, edge_w1_grad, edge_w2_grad)
        e_copies = across_x(ebuf, ep1, e1_s, e1_r)
        e_rest = (e_copies, ebuf, ep1, esum, ep2)
        along_z(2, *n_rest, n2_s, n2_r)
    else:
        ew1_out[...] = edge_w1_grad
        ew2_out[...] = edge_w2_grad

    per_code = nt(by_code, w1_ref[width : 2 * width])
    back_out[...] = per_code[nodes:codes]
    backs = []
    for k in range(neigh):
        block = pl.ds(k * slots, slots)
        copy = remote(
            back_out.at[block], back_in.at[block], back_s.at[k], back_r.at[k],
            at(-offset_of(k, half)),
        )
        copy.start()
        backs.append(copy)
    edge_trades = []
    for c in range(CHUNKS):
        r = pl.ds(c * rows, rows)
        dmine[r] = nt(dpre[r], w1_ref[0:width]).astype(BF)
        s = CHUNKS + 2 + c
        copy = remote(dmine.at[r], dtheirs.at[r], mp_s.at[s], mp_r.at[s], other)
        copy.start()
        edge_trades.append(copy)
    node_own = node_own + per_code[0:nodes] + nt(by_node, w1_ref[2 * width : 3 * width])
    if scatter:
        along_z(0, *e_rest, e2_s, e2_r)
    for copy in backs:
        copy.wait_recv()
    fmine[...] = node_own + nn(lists, back_in[...].astype(BF))
    last = 2 * CHUNKS + 2
    final = remote(fmine, ftheirs, mp_s.at[last], mp_r.at[last], other)
    final.start()
    if scatter:
        along_z(1, *e_rest, e2_s, e2_r)
    for c in range(CHUNKS):
        r = pl.ds(c * rows, rows)
        edge_trades[c].wait_recv()
        total = dmine[r].astype(F32) + dtheirs[r].astype(F32)
        egrad_ref[r] = (live[r] * (ecot_ref[r].astype(F32) + total)).astype(BF)
    if scatter:
        along_z(2, *e_rest, e2_s, e2_r)
    stores = [load(12, egrad_ref, egrad_hbm)]
    final.wait_recv()
    ngrad_ref[...] = (ncot_ref[...].astype(F32) + fmine[...] + ftheirs[...]).astype(BF)
    stores.append(load(11, ngrad_ref, ngrad_hbm))
    if scatter:
        finish(*n_rest, nw1_out, nw2_out)
    stores.append(load(15, nw1_out, nw1_grad_hbm))
    stores.append(load(16, nw2_out, nw2_grad_hbm))
    if scatter:
        finish(*e_rest, ew1_out, ew2_out)
    stores.append(load(13, ew1_out, ew1_hbm))
    stores.append(load(14, ew2_out, ew2_hbm))
    if scatter:
        for copy in n_copies + e_copies:
            copy.wait_send()
    for copy in halo + trades + backs + edge_trades + [final]:
        copy.wait_send()
    for copy in stores:
        copy.wait()


def write_kernel(*refs):
    copies = []
    for index in range(6):
        copy = pltpu.make_async_copy(refs[index], refs[6 + index], refs[12].at[index])
        copy.start()
        copies.append(copy)
    for copy in copies:
        copy.wait()


def write_out(*results):
    return pl.pallas_call(
        write_kernel,
        out_shape=[jax.ShapeDtypeStruct(v.shape, v.dtype) for v in results],
        in_specs=[pl.BlockSpec(memory_space=pltpu.HBM)] * 6,
        out_specs=[pl.BlockSpec(memory_space=pltpu.HBM)] * 6,
        scratch_shapes=[pltpu.SemaphoreType.DMA((6,))],
        compiler_params=pltpu.CompilerParams(vmem_limit_bytes=VMEM_LIMIT),
    )(*results)


def local(
    count,
    node_latent,
    edge_latent,
    node_cot,
    edge_cot,
    edge_w1,
    edge_w2,
    node_w1,
    node_w2,
    send_rows,
    edge_sender,
    edge_receiver,
    edge_count,
):
    nodes, width = node_latent.shape
    edges = edge_latent.shape[0]
    hidden = edge_w1.shape[1]
    neigh, slots = send_rows.shape[1:]
    listed = neigh * slots
    codes = nodes + listed
    total = -(-(codes + nodes) // 128) * 128
    w1_rows, nw1_rows = edge_w1.shape[0], node_w1.shape[0]
    scatter = (
        count == 8
        and w1_rows % (16 * count) == 0
        and nw1_rows % (16 * count) == 0
        and width % (16 * count) == 0
    )
    parts = count if scatter else 1
    n_rows = (nw1_rows + width) // parts if scatter else 16
    e_rows = (w1_rows + width) // parts if scatter else 16
    vmem = pltpu.VMEM
    dma = pltpu.SemaphoreType.DMA
    scratch = [
        vmem((nodes, width), BF),
        vmem((edges, width), BF),
        vmem((nodes, width), BF),
        vmem((edges, width), BF),
        vmem(edge_w1.shape, BF),
        vmem(edge_w2.shape, BF),
        vmem(node_w1.shape, BF),
        vmem(node_w2.shape, BF),
        vmem((neigh, 1, slots), jnp.int32),
        vmem((edges,), jnp.int32),
        vmem((edges,), jnp.int32),
        vmem((nodes, listed), F32),
        vmem((total, edges), BF),
        vmem((edges, total), BF),
        vmem((edges, 1), F32),
        vmem((listed, width), F32),
        vmem((listed, width), F32),
        vmem((codes, width), BF),
        vmem((total, hidden), BF),
        vmem((edges, hidden), F32),
        vmem((edges, hidden), BF),
        vmem((edges, hidden), F32),
        vmem((edges, width), BF),
        vmem((edges, width), BF),
        vmem((edges, width), F32),
        vmem((edges, 1), F32),
        vmem((edges, width), BF),
        vmem((nodes, width), BF),
        vmem((nodes, width), BF),
        vmem((nodes, width), BF),
        vmem((nodes, width), BF),
        vmem((edges, width), BF),
        vmem((edges, hidden), BF),
        vmem((edges, width), BF),
        vmem((edges, width), BF),
        vmem((listed, width), F32),
        vmem((listed, width), F32),
        vmem((nodes, width), F32),
        vmem((nodes, width), F32),
        vmem((2, 4, n_rows, hidden), BF),
        vmem((4, n_rows, hidden), BF),
        vmem((3, n_rows, hidden), BF),
        vmem((3, n_rows, hidden), BF),
        vmem((2, 4, e_rows, hidden), BF),
        vmem((4, e_rows, hidden), BF),
        vmem((3, e_rows, hidden), BF),
        vmem((3, e_rows, hidden), BF),
        dma((neigh,)),
        dma((neigh,)),
        dma((neigh,)),
        dma((neigh,)),
        dma((2 * CHUNKS + 3,)),
        dma((2 * CHUNKS + 3,)),
        dma((4,)),
        dma((4,)),
        dma((3,)),
        dma((3,)),
        dma((4,)),
        dma((4,)),
        dma((3,)),
        dma((3,)),
        dma((17,)),
    ]
    shape = jax.ShapeDtypeStruct
    shapes = (
        shape((nodes, width), BF),
        shape((edges, width), BF),
        shape((w1_rows // parts, hidden), F32),
        shape((width // parts, hidden), F32),
        shape((nw1_rows // parts, hidden), F32),
        shape((width // parts, hidden), F32),
    )
    node_grad, edge_grad, ew1, ew2, nw1, nw2 = pl.pallas_call(
        functools.partial(kernel, (count, neigh, slots, scatter)),
        out_shape=shapes,
        in_specs=[pl.BlockSpec(memory_space=pltpu.HBM)] * 11
        + [pl.BlockSpec(memory_space=pltpu.SMEM)],
        out_specs=[pl.BlockSpec(memory_space=pltpu.HBM)] * 6,
        scratch_shapes=[vmem(v.shape, v.dtype) for v in shapes] + scratch,
        compiler_params=pltpu.CompilerParams(
            collective_id=0, has_side_effects=True, vmem_limit_bytes=VMEM_LIMIT
        ),
    )(
        node_latent, edge_latent, node_cot, edge_cot, edge_w1, edge_w2, node_w1, node_w2,
        jnp.transpose(send_rows, (1, 0, 2)), edge_sender, edge_receiver, edge_count,
    )
    if scatter:
        node_grad, edge_grad, ew1, ew2, nw1, nw2 = write_out(
            node_grad, edge_grad, ew1, ew2, nw1, nw2
        )
        return node_grad, edge_grad, ew1, ew2.T, nw1, nw2.T
    ew2, nw2 = ew2.T, nw2.T
    ew1, nw1 = (lax.psum_scatter(g, "dom", scatter_dimension=0, tiled=True) for g in (ew1, nw1))
    ew2, nw2 = (lax.psum_scatter(g, "dom", scatter_dimension=1, tiled=True) for g in (ew2, nw2))
    return node_grad, edge_grad, ew1, ew2, nw1, nw2


def solution(mesh):
    placed = (
        P(("groups", "dom"), None),
        P(("groups", "dom"), None),
        P(("groups", "dom"), None),
        P(("groups", "dom"), None),
        P(None, "mp"),
        P("mp", None),
        P(None, "mp"),
        P("mp", None),
        P("dom", None, None),
        P("dom"),
        P("dom"),
        P("dom"),
    )
    return jax.shard_map(
        functools.partial(local, mesh.shape["dom"]),
        mesh=mesh,
        in_specs=placed,
        out_specs=(
            P(("groups", "dom"), None),
            P(("groups", "dom"), None),
            P(("groups", "dom"), "mp"),
            P(("groups", "mp"), "dom"),
            P(("groups", "dom"), "mp"),
            P(("groups", "mp"), "dom"),
        ),
        check_vma=False,
    )
```

```python
import functools

import jax
import jax.numpy as jnp
from jax import lax
from jax.experimental import pallas as pl
from jax.experimental.pallas import tpu as pltpu
from jax.sharding import PartitionSpec as P

EPS = 1e-05
BF = jnp.bfloat16
F32 = jnp.float32
MESH = pl.DeviceIdType.MESH
CHUNKS = 3
VMEM_LIMIT = 62 * 1024 * 1024


def dot(left, right, contract):
    return lax.dot_general(
        left, right, (((contract[0],), (contract[1],)), ((), ())), preferred_element_type=F32
    )


def nn(left, right):
    return dot(left, right, (1, 0))


def nt(left, right):
    return dot(left, right, (1, 1))


def tn(left, right):
    return dot(left, right, (0, 0))


def layer_norm(values):
    center = values - jnp.mean(values, axis=-1, keepdims=True)
    inverse = lax.rsqrt(jnp.mean(center * center, axis=-1, keepdims=True) + EPS)
    return (center * inverse, inverse)


def norm_back(normed, inverse, upstream):
    first = jnp.mean(upstream, axis=-1, keepdims=True)
    second = jnp.mean(upstream * normed, axis=-1, keepdims=True)
    return inverse * (upstream - first - normed * second)


def silu_and_slope(values):
    sigma = jax.nn.sigmoid(values)
    return values * sigma, sigma * (1.0 + values * (1.0 - sigma))


def offset_of(index, half):
    return (index % half + 1) * (1 if index < half else -1)


def kernel(
    dims,
    node_hbm,
    edge_hbm,
    ncot_hbm,
    ecot_hbm,
    w1_hbm,
    w2_hbm,
    nw1_hbm,
    nw2_hbm,
    send_hbm,
    sender_hbm,
    receiver_hbm,
    count_ref,
    ngrad_hbm,
    egrad_hbm,
    ew1_hbm,
    ew2_hbm,
    nw1_grad_hbm,
    nw2_grad_hbm,
    ngrad_ref,
    egrad_ref,
    ew1_out,
    ew2_out,
    nw1_out,
    nw2_out,
    node_ref,
    edge_ref,
    ncot_ref,
    ecot_ref,
    w1_ref,
    w2_ref,
    nw1_ref,
    nw2_ref,
    send_ref,
    sender_ref,
    receiver_ref,
    lists_ref,
    pick,
    pick_t,
    live,
    halo_out,
    halo_in,
    sources,
    table,
    pre,
    act,
    slope,
    mine,
    theirs,
    normed,
    inverse,
    upd,
    nmine,
    ntheirs,
    gmine,
    gtheirs,
    dout,
    dpre,
    dmine,
    dtheirs,
    back_out,
    back_in,
    fmine,
    ftheirs,
    rs_refs,
    halo_s,
    halo_r,
    back_s,
    back_r,
    mp_s,
    mp_r,
    rs_s,
    rs_r,
    load_s,
):
    count, neigh, slots, scatter = dims
    me = lax.axis_index("dom")
    core = lax.axis_index("mp")
    other = {"mp": 1 - core}
    nodes, width = node_ref.shape
    edges = edge_ref.shape[0]
    hidden = w2_ref.shape[0]
    listed = neigh * slots
    codes = nodes + listed
    rows = edges // CHUNKS
    half = neigh // 2

    def at(shift):
        return {"dom": lax.rem(me + shift + count, count)}

    def remote(src, dst, send, recv, device):
        return pltpu.make_async_remote_copy(
            src_ref=src,
            dst_ref=dst,
            send_sem=send,
            recv_sem=recv,
            device_id=device,
            device_id_type=MESH,
        )

    def load(index, src, dst):
        copy = pltpu.make_async_copy(src, dst, load_s.at[index])
        copy.start()
        return copy

    loads = [
        load(0, send_hbm, send_ref),
        load(1, node_hbm, node_ref),
        load(2, sender_hbm, sender_ref),
        load(3, receiver_hbm, receiver_ref),
        load(4, edge_hbm, edge_ref),
        load(5, w1_hbm, w1_ref),
        load(6, w2_hbm, w2_ref),
        load(7, nw1_hbm, nw1_ref),
        load(8, nw2_hbm, nw2_ref),
        load(9, ncot_hbm, ncot_ref),
        load(10, ecot_hbm, ecot_ref),
    ]
    barrier = pltpu.get_barrier_semaphore()
    shifts = sorted({offset_of(k, half) % count for k in range(neigh)})
    shifts = sorted(set(shifts) | {(-s) % count for s in shifts})
    if scatter:
        shifts = list(range(1, count))
    for shift in shifts:
        pl.semaphore_signal(barrier, inc=1, device_id=at(shift), device_id_type=MESH)
    pl.semaphore_signal(barrier, inc=1, device_id=other, device_id_type=MESH)

    send_place = lax.broadcasted_iota(jnp.int32, (nodes, slots), 0)
    loads[0].wait()
    for k in range(neigh):
        hit = send_place == send_ref[k]
        lists_ref[:, k * slots : (k + 1) * slots] = jnp.where(hit, 1.0, 0.0).astype(F32)
    lists = lists_ref[...].astype(BF)
    loads[1].wait()
    node = node_ref[...]
    halo_out[...] = tn(lists, node)
    loads[2].wait()
    loads[3].wait()
    place = lax.broadcasted_iota(jnp.int32, pick.shape, 0)
    alive = lax.broadcasted_iota(jnp.int32, pick.shape, 1) < count_ref[0]
    hit = (place == sender_ref[...][None, :]) | (place == receiver_ref[...][None, :] + codes)
    pick_f = jnp.where(hit & alive, 1.0, 0.0).astype(F32)
    pick[...] = pick_f.astype(BF)

    pl.semaphore_wait(barrier, len(shifts) + 1)
    halo = []
    for k in range(neigh):
        block = pl.ds(k * slots, slots)
        copy = remote(
            halo_out.at[block], halo_in.at[block], halo_s.at[k], halo_r.at[k],
            at(offset_of(k, half)),
        )
        copy.start()
        halo.append(copy)

    picked = jnp.transpose(pick_f)
    pick_t[...] = picked.astype(BF)
    live[...] = jnp.max(picked, axis=1, keepdims=True)
    loads[4].wait()
    loads[5].wait()
    pre[...] = nn(edge_ref[...], w1_ref[0:width])
    table[0:nodes] = nn(node, w1_ref[width : 2 * width]).astype(BF)
    table[codes : codes + nodes] = nn(node, w1_ref[2 * width : 3 * width]).astype(BF)
    if pick.shape[0] > codes + nodes:
        table[codes + nodes :] = jnp.zeros((pick.shape[0] - codes - nodes, hidden), BF)
    sources[0:nodes] = node
    for copy in halo:
        copy.wait_recv()
    arrived = halo_in[...].astype(BF)
    sources[nodes:codes] = arrived
    table[nodes:codes] = nn(arrived, w1_ref[width : 2 * width]).astype(BF)

    loads[6].wait()
    trades = []
    for c in range(CHUNKS):
        r = pl.ds(c * rows, rows)
        values = pre[r] + nn(pick_t[r], table[...])
        a, s = silu_and_slope(values)
        a = a.astype(BF)
        act[r] = a
        slope[r] = s
        mine[r] = nn(a, w2_ref[...]).astype(BF)
        copy = remote(mine.at[r], theirs.at[r], mp_s.at[c], mp_r.at[c], other)
        copy.start()
        trades.append(copy)
    for copy in loads[7:]:
        copy.wait()
    node_first = nn(node, nw1_ref[0:width])
    for c in range(CHUNKS):
        r = pl.ds(c * rows, rows)
        trades[c].wait_recv()
        n, i = layer_norm(mine[r].astype(F32) + theirs[r].astype(F32))
        normed[r] = n
        inverse[r] = i
        upd[r] = n.astype(BF)
    gathered = nn(pick[codes : codes + nodes], upd[...]).astype(BF)

    node_act, node_slope = silu_and_slope(node_first + nn(gathered, nw1_ref[width : 2 * width]))
    node_act = node_act.astype(BF)
    nmine[...] = nn(node_act, nw2_ref[...]).astype(BF)
    trade = remote(nmine, ntheirs, mp_s.at[CHUNKS], mp_r.at[CHUNKS], other)
    trade.start()
    trades.append(trade)
    trade.wait_recv()
    n, i = layer_norm(nmine[...].astype(F32) + ntheirs[...].astype(F32))
    node_dout = norm_back(n, i, ncot_ref[...].astype(F32)).astype(BF)
    node_dpre = (nt(node_dout, nw2_ref[...]) * node_slope).astype(BF)
    gmine[...] = nt(node_dpre, nw1_ref[width : 2 * width]).astype(BF)
    trade = remote(gmine, gtheirs, mp_s.at[CHUNKS + 1], mp_r.at[CHUNKS + 1], other)
    trade.start()
    trades.append(trade)

    x = lax.rem(me, 2)
    z = lax.div(me, 2)
    near = z + 1 - 2 * lax.rem(z, 2)
    far = lax.rem(z + 2, 4)
    both = lax.rem(near + 2, 4)

    def spot(flips):
        along = {"": z, "0": near, "1": far, "01": both}
        return (1 - x if "x" in flips else x), along["".join(sorted(set(flips) - {"x"}))]

    def device(flips):
        across, along = spot(flips)
        return {"dom": along * 2 + across}

    routes = ("x01", "0x1", "x01", "0x1")

    def owners(which):
        first, second, third = routes[which]
        return first, second, third, (second + third, second, third, "")

    def first_hop(which, grad):
        buf, land = rs_refs[which][:2]
        size = grad.shape[0] // count
        for j in range(count):
            buf[j % 2, j // 2] = grad[j * size : (j + 1) * size].astype(BF)
        first, _, _, slices = owners(which)
        copies = []
        for k in range(4):
            copy = remote(
                buf.at[spot(first + slices[k])], land.at[k],
                rs_s.at[which, k], rs_r.at[which, k], device(first),
            )
            copy.start()
            copies.append(copy)
        sums[which] = copies

    def next_hop(which, k):
        copies = sums[which]
        buf, land, summed, land2 = rs_refs[which]
        _, second, third, slices = owners(which)
        copies[k].wait_recv()
        total = buf[spot(slices[k])].astype(F32) + land[k].astype(F32)
        if k == 2:
            copies[4].wait_recv()
            total = total + land2[0].astype(F32)
        summed[k] = total.astype(BF)
        copy = remote(
            summed.at[k], land2.at[k], rs_s.at[which, 4 + k], rs_r.at[which, 4 + k],
            device(second if k < 2 else third),
        )
        copy.start()
        copies.append(copy)

    def finish(which, out):
        copies = sums[which]
        buf, land, summed, land2 = rs_refs[which]
        copies[3].wait_recv()
        copies[5].wait_recv()
        total = buf[x, z].astype(F32) + land[3].astype(F32) + land2[1].astype(F32)
        copies[6].wait_recv()
        out[...] = total + land2[2].astype(F32)

    sums = {}
    node_w2_grad = tn(node_dout, node_act)
    if scatter:
        first_hop(1, node_w2_grad)
    node_w1_grad = jnp.concatenate([tn(node, node_dpre), tn(gathered, node_dpre)], axis=0)
    if scatter:
        first_hop(0, node_w1_grad)
    else:
        nw1_out[...] = node_w1_grad
        nw2_out[...] = node_w2_grad
    node_own = nt(node_dpre, nw1_ref[0:width])

    trade.wait_recv()
    gathered_grad = (gmine[...].astype(F32) + gtheirs[...].astype(F32)).astype(BF)
    for c in range(CHUNKS):
        r = pl.ds(c * rows, rows)
        upstream = live[r] * ecot_ref[r].astype(F32) + nn(
            pick_t[r, codes : codes + nodes], gathered_grad
        )
        d = norm_back(normed[r], inverse[r], upstream).astype(BF)
        dout[r] = d
        dpre[r] = (nt(d, w2_ref[...]) * slope[r]).astype(BF)
        if scatter and c > 0:
            next_hop(1, c - 1)
            next_hop(0, c - 1)
    edge_w2_grad = tn(dout[...], act[...])
    if scatter:
        first_hop(3, edge_w2_grad)
    merged = nn(pick[...], dpre[...]).astype(BF)
    by_code = merged[0:codes]
    by_node = merged[codes : codes + nodes]
    edge_w1_grad = jnp.concatenate(
        [tn(edge_ref[...], dpre[...]), tn(sources[...], by_code), tn(node, by_node)], axis=0
    )
    if scatter:
        first_hop(2, edge_w1_grad)
        next_hop(1, 2)
        next_hop(0, 2)
    else:
        ew1_out[...] = edge_w1_grad
        ew2_out[...] = edge_w2_grad

    per_code = nt(by_code, w1_ref[width : 2 * width])
    back_out[...] = per_code[nodes:codes]
    backs = []
    for k in range(neigh):
        block = pl.ds(k * slots, slots)
        copy = remote(
            back_out.at[block], back_in.at[block], back_s.at[k], back_r.at[k],
            at(-offset_of(k, half)),
        )
        copy.start()
        backs.append(copy)
    edge_trades = []
    for c in range(CHUNKS):
        r = pl.ds(c * rows, rows)
        dmine[r] = nt(dpre[r], w1_ref[0:width]).astype(BF)
        s = CHUNKS + 2 + c
        copy = remote(dmine.at[r], dtheirs.at[r], mp_s.at[s], mp_r.at[s], other)
        copy.start()
        edge_trades.append(copy)
    node_own = node_own + per_code[0:nodes] + nt(by_node, w1_ref[2 * width : 3 * width])
    if scatter:
        next_hop(3, 0)
        next_hop(2, 0)
    for copy in backs:
        copy.wait_recv()
    fmine[...] = node_own + nn(lists, back_in[...].astype(BF))
    last = 2 * CHUNKS + 2
    final = remote(fmine, ftheirs, mp_s.at[last], mp_r.at[last], other)
    final.start()
    if scatter:
        next_hop(3, 1)
        next_hop(2, 1)
    for c in range(CHUNKS):
        r = pl.ds(c * rows, rows)
        edge_trades[c].wait_recv()
        total = dmine[r].astype(F32) + dtheirs[r].astype(F32)
        egrad_ref[r] = (live[r] * (ecot_ref[r].astype(F32) + total)).astype(BF)
    if scatter:
        next_hop(3, 2)
        next_hop(2, 2)
    stores = [load(12, egrad_ref, egrad_hbm)]
    final.wait_recv()
    ngrad_ref[...] = (ncot_ref[...].astype(F32) + fmine[...] + ftheirs[...]).astype(BF)
    stores.append(load(11, ngrad_ref, ngrad_hbm))
    if scatter:
        finish(1, nw2_out)
        finish(0, nw1_out)
    stores.append(load(15, nw1_out, nw1_grad_hbm))
    stores.append(load(16, nw2_out, nw2_grad_hbm))
    if scatter:
        finish(3, ew2_out)
        finish(2, ew1_out)
    stores.append(load(13, ew1_out, ew1_hbm))
    stores.append(load(14, ew2_out, ew2_hbm))
    if scatter:
        for copy in sums[0] + sums[1] + sums[2] + sums[3]:
            copy.wait_send()
    for copy in halo + trades + backs + edge_trades + [final]:
        copy.wait_send()
    for copy in stores:
        copy.wait()


def write_kernel(*refs):
    ins, outs, held, sems = refs[:6], refs[6:12], refs[12:18], refs[18]
    order = (1, 2, 4, 0, 3, 5)
    copies = {}
    for index in order:
        copies[index] = pltpu.make_async_copy(ins[index], held[index], sems.at[0, index])
        copies[index].start()
    stores = []
    for index in order:
        copies[index].wait()
        store = pltpu.make_async_copy(held[index], outs[index], sems.at[1, index])
        store.start()
        stores.append(store)
    for store in stores:
        store.wait()


def write_out(*results):
    return pl.pallas_call(
        write_kernel,
        out_shape=[jax.ShapeDtypeStruct(v.shape, v.dtype) for v in results],
        in_specs=[pl.BlockSpec(memory_space=pltpu.HBM)] * 6,
        out_specs=[pl.BlockSpec(memory_space=pltpu.HBM)] * 6,
        scratch_shapes=[pltpu.VMEM(v.shape, v.dtype) for v in results]
        + [pltpu.SemaphoreType.DMA((2, 6))],
        compiler_params=pltpu.CompilerParams(vmem_limit_bytes=VMEM_LIMIT),
    )(*results)


def local(
    count,
    node_latent,
    edge_latent,
    node_cot,
    edge_cot,
    edge_w1,
    edge_w2,
    node_w1,
    node_w2,
    send_rows,
    edge_sender,
    edge_receiver,
    edge_count,
):
    nodes, width = node_latent.shape
    edges = edge_latent.shape[0]
    hidden = edge_w1.shape[1]
    neigh, slots = send_rows.shape[1:]
    listed = neigh * slots
    codes = nodes + listed
    total = -(-(codes + nodes) // 128) * 128
    w1_rows, nw1_rows = edge_w1.shape[0], node_w1.shape[0]
    scatter = (
        count == 8
        and w1_rows % (16 * count) == 0
        and nw1_rows % (16 * count) == 0
        and width % (16 * count) == 0
    )
    parts = count if scatter else 1
    sizes = [r // parts if scatter else 16 for r in (nw1_rows, width, w1_rows, width)]
    vmem = pltpu.VMEM
    dma = pltpu.SemaphoreType.DMA
    scratch = [
        vmem((nodes, width), BF),
        vmem((edges, width), BF),
        vmem((nodes, width), BF),
        vmem((edges, width), BF),
        vmem(edge_w1.shape, BF),
        vmem(edge_w2.shape, BF),
        vmem(node_w1.shape, BF),
        vmem(node_w2.shape, BF),
        vmem((neigh, 1, slots), jnp.int32),
        vmem((edges,), jnp.int32),
        vmem((edges,), jnp.int32),
        vmem((nodes, listed), F32),
        vmem((total, edges), BF),
        vmem((edges, total), BF),
        vmem((edges, 1), F32),
        vmem((listed, width), F32),
        vmem((listed, width), F32),
        vmem((codes, width), BF),
        vmem((total, hidden), BF),
        vmem((edges, hidden), F32),
        vmem((edges, hidden), BF),
        vmem((edges, hidden), F32),
        vmem((edges, width), BF),
        vmem((edges, width), BF),
        vmem((edges, width), F32),
        vmem((edges, 1), F32),
        vmem((edges, width), BF),
        vmem((nodes, width), BF),
        vmem((nodes, width), BF),
        vmem((nodes, width), BF),
        vmem((nodes, width), BF),
        vmem((edges, width), BF),
        vmem((edges, hidden), BF),
        vmem((edges, width), BF),
        vmem((edges, width), BF),
        vmem((listed, width), F32),
        vmem((listed, width), F32),
        vmem((nodes, width), F32),
        vmem((nodes, width), F32),
        [
            (
                vmem((2, 4, size, hidden), BF),
                vmem((4, size, hidden), BF),
                vmem((3, size, hidden), BF),
                vmem((3, size, hidden), BF),
            )
            for size in sizes
        ],
        dma((neigh,)),
        dma((neigh,)),
        dma((neigh,)),
        dma((neigh,)),
        dma((2 * CHUNKS + 3,)),
        dma((2 * CHUNKS + 3,)),
        dma((4, 7)),
        dma((4, 7)),
        dma((17,)),
    ]
    shape = jax.ShapeDtypeStruct
    shapes = (
        shape((nodes, width), BF),
        shape((edges, width), BF),
        shape((w1_rows // parts, hidden), F32),
        shape((width // parts, hidden), F32),
        shape((nw1_rows // parts, hidden), F32),
        shape((width // parts, hidden), F32),
    )
    node_grad, edge_grad, ew1, ew2, nw1, nw2 = pl.pallas_call(
        functools.partial(kernel, (count, neigh, slots, scatter)),
        out_shape=shapes,
        in_specs=[pl.BlockSpec(memory_space=pltpu.HBM)] * 11
        + [pl.BlockSpec(memory_space=pltpu.SMEM)],
        out_specs=[pl.BlockSpec(memory_space=pltpu.HBM)] * 6,
        scratch_shapes=[vmem(v.shape, v.dtype) for v in shapes] + scratch,
        compiler_params=pltpu.CompilerParams(
            collective_id=0, has_side_effects=True, vmem_limit_bytes=VMEM_LIMIT
        ),
    )(
        node_latent, edge_latent, node_cot, edge_cot, edge_w1, edge_w2, node_w1, node_w2,
        jnp.transpose(send_rows, (1, 0, 2)), edge_sender, edge_receiver, edge_count,
    )
    if scatter:
        node_grad, edge_grad, ew1, ew2, nw1, nw2 = write_out(
            node_grad, edge_grad, ew1, ew2, nw1, nw2
        )
        return node_grad, edge_grad, ew1, ew2.T, nw1, nw2.T
    ew2, nw2 = ew2.T, nw2.T
    ew1, nw1 = (lax.psum_scatter(g, "dom", scatter_dimension=0, tiled=True) for g in (ew1, nw1))
    ew2, nw2 = (lax.psum_scatter(g, "dom", scatter_dimension=1, tiled=True) for g in (ew2, nw2))
    return node_grad, edge_grad, ew1, ew2, nw1, nw2


def solution(mesh):
    placed = (
        P(("groups", "dom"), None),
        P(("groups", "dom"), None),
        P(("groups", "dom"), None),
        P(("groups", "dom"), None),
        P(None, "mp"),
        P("mp", None),
        P(None, "mp"),
        P("mp", None),
        P("dom", None, None),
        P("dom"),
        P("dom"),
        P("dom"),
    )
    return jax.shard_map(
        functools.partial(local, mesh.shape["dom"]),
        mesh=mesh,
        in_specs=placed,
        out_specs=(
            P(("groups", "dom"), None),
            P(("groups", "dom"), None),
            P(("groups", "dom"), "mp"),
            P(("groups", "mp"), "dom"),
            P(("groups", "dom"), "mp"),
            P(("groups", "mp"), "dom"),
        ),
        check_vma=False,
    )
```

```python
import functools

import jax
import jax.numpy as jnp
from jax import lax
from jax.experimental import pallas as pl
from jax.experimental.pallas import tpu as pltpu
from jax.sharding import PartitionSpec as P

EPS = 1e-05
BF = jnp.bfloat16
F32 = jnp.float32
MESH = pl.DeviceIdType.MESH
CHUNKS = 3
VMEM_LIMIT = 62 * 1024 * 1024


def dot(left, right, contract):
    return lax.dot_general(
        left, right, (((contract[0],), (contract[1],)), ((), ())), preferred_element_type=F32
    )


def nn(left, right):
    return dot(left, right, (1, 0))


def nt(left, right):
    return dot(left, right, (1, 1))


def tn(left, right):
    return dot(left, right, (0, 0))


def layer_norm(values):
    center = values - jnp.mean(values, axis=-1, keepdims=True)
    inverse = lax.rsqrt(jnp.mean(center * center, axis=-1, keepdims=True) + EPS)
    return (center * inverse, inverse)


def norm_back(normed, inverse, upstream):
    first = jnp.mean(upstream, axis=-1, keepdims=True)
    second = jnp.mean(upstream * normed, axis=-1, keepdims=True)
    return inverse * (upstream - first - normed * second)


def silu_and_slope(values):
    sigma = jax.nn.sigmoid(values)
    return values * sigma, sigma * (1.0 + values * (1.0 - sigma))


def offset_of(index, half):
    return (index % half + 1) * (1 if index < half else -1)


def kernel(
    dims,
    node_hbm,
    edge_hbm,
    ncot_hbm,
    ecot_hbm,
    w1_hbm,
    w2_hbm,
    nw1_hbm,
    nw2_hbm,
    send_hbm,
    sender_hbm,
    receiver_hbm,
    count_ref,
    ngrad_hbm,
    egrad_hbm,
    ew1_hbm,
    ew2_hbm,
    nw1_grad_hbm,
    nw2_grad_hbm,
    ngrad_ref,
    egrad_ref,
    ew1_out,
    ew2_out,
    nw1_out,
    nw2_out,
    node_ref,
    edge_ref,
    ncot_ref,
    ecot_ref,
    w1_ref,
    w2_ref,
    nw1_ref,
    nw2_ref,
    send_ref,
    sender_ref,
    receiver_ref,
    lists_ref,
    pick,
    pick_t,
    live,
    halo_out,
    halo_in,
    sources,
    table,
    pre,
    act,
    slope,
    mine,
    theirs,
    normed,
    inverse,
    upd,
    nmine,
    ntheirs,
    gmine,
    gtheirs,
    dout,
    dpre,
    dmine,
    dtheirs,
    back_out,
    back_in,
    fmine,
    ftheirs,
    rs_refs,
    halo_s,
    halo_r,
    back_s,
    back_r,
    mp_s,
    mp_r,
    rs_s,
    rs_r,
    load_s,
):
    count, neigh, slots, scatter = dims
    me = lax.axis_index("dom")
    core = lax.axis_index("mp")
    other = {"mp": 1 - core}
    nodes, width = node_ref.shape
    edges = edge_ref.shape[0]
    hidden = w2_ref.shape[0]
    listed = neigh * slots
    codes = nodes + listed
    rows = edges // CHUNKS
    half = neigh // 2

    def at(shift):
        return {"dom": lax.rem(me + shift + count, count)}

    def remote(src, dst, send, recv, device):
        return pltpu.make_async_remote_copy(
            src_ref=src,
            dst_ref=dst,
            send_sem=send,
            recv_sem=recv,
            device_id=device,
            device_id_type=MESH,
        )

    def load(index, src, dst):
        copy = pltpu.make_async_copy(src, dst, load_s.at[index])
        copy.start()
        return copy

    loads = [
        load(0, send_hbm, send_ref),
        load(1, node_hbm, node_ref),
        load(2, sender_hbm, sender_ref),
        load(3, receiver_hbm, receiver_ref),
        load(4, edge_hbm, edge_ref),
        load(5, w1_hbm, w1_ref),
        load(6, w2_hbm, w2_ref),
        load(7, nw1_hbm, nw1_ref),
        load(8, nw2_hbm, nw2_ref),
        load(9, ncot_hbm, ncot_ref),
        load(10, ecot_hbm, ecot_ref),
    ]
    barrier = pltpu.get_barrier_semaphore()
    shifts = sorted({offset_of(k, half) % count for k in range(neigh)})
    shifts = sorted(set(shifts) | {(-s) % count for s in shifts})
    if scatter:
        shifts = list(range(1, count))
    for shift in shifts:
        pl.semaphore_signal(barrier, inc=1, device_id=at(shift), device_id_type=MESH)
    pl.semaphore_signal(barrier, inc=1, device_id=other, device_id_type=MESH)

    send_place = lax.broadcasted_iota(jnp.int32, (nodes, slots), 0)
    loads[0].wait()
    for k in range(neigh):
        hit = send_place == send_ref[k]
        lists_ref[:, k * slots : (k + 1) * slots] = jnp.where(hit, 1.0, 0.0).astype(F32)
    lists = lists_ref[...].astype(BF)
    loads[1].wait()
    node = node_ref[...]
    halo_out[...] = tn(lists, node)
    loads[2].wait()
    loads[3].wait()
    place = lax.broadcasted_iota(jnp.int32, pick.shape, 0)
    alive = lax.broadcasted_iota(jnp.int32, pick.shape, 1) < count_ref[0]
    hit = (place == sender_ref[...][None, :]) | (place == receiver_ref[...][None, :] + codes)
    pick_f = jnp.where(hit & alive, 1.0, 0.0).astype(F32)
    pick[...] = pick_f.astype(BF)

    pl.semaphore_wait(barrier, len(shifts) + 1)
    halo = []
    for k in range(neigh):
        block = pl.ds(k * slots, slots)
        copy = remote(
            halo_out.at[block], halo_in.at[block], halo_s.at[k], halo_r.at[k],
            at(offset_of(k, half)),
        )
        copy.start()
        halo.append(copy)

    picked = jnp.transpose(pick_f)
    pick_t[...] = picked.astype(BF)
    live[...] = jnp.max(picked, axis=1, keepdims=True)
    loads[4].wait()
    loads[5].wait()
    pre[...] = nn(edge_ref[...], w1_ref[0:width])
    table[0:nodes] = nn(node, w1_ref[width : 2 * width]).astype(BF)
    table[codes : codes + nodes] = nn(node, w1_ref[2 * width : 3 * width]).astype(BF)
    if pick.shape[0] > codes + nodes:
        table[codes + nodes :] = jnp.zeros((pick.shape[0] - codes - nodes, hidden), BF)
    sources[0:nodes] = node
    for copy in halo:
        copy.wait_recv()
    arrived = halo_in[...].astype(BF)
    sources[nodes:codes] = arrived
    table[nodes:codes] = nn(arrived, w1_ref[width : 2 * width]).astype(BF)

    loads[6].wait()
    trades = []
    for c in range(CHUNKS):
        r = pl.ds(c * rows, rows)
        values = pre[r] + nn(pick_t[r], table[...])
        a, s = silu_and_slope(values)
        a = a.astype(BF)
        act[r] = a
        slope[r] = s
        mine[r] = nn(a, w2_ref[...]).astype(BF)
        copy = remote(mine.at[r], theirs.at[r], mp_s.at[c], mp_r.at[c], other)
        copy.start()
        trades.append(copy)
    for copy in loads[7:]:
        copy.wait()
    node_first = nn(node, nw1_ref[0:width])
    for c in range(CHUNKS):
        r = pl.ds(c * rows, rows)
        trades[c].wait_recv()
        n, i = layer_norm(mine[r].astype(F32) + theirs[r].astype(F32))
        normed[r] = n
        inverse[r] = i
        upd[r] = n.astype(BF)
    gathered = nn(pick[codes : codes + nodes], upd[...]).astype(BF)

    node_act, node_slope = silu_and_slope(node_first + nn(gathered, nw1_ref[width : 2 * width]))
    node_act = node_act.astype(BF)
    nmine[...] = nn(node_act, nw2_ref[...]).astype(BF)
    trade = remote(nmine, ntheirs, mp_s.at[CHUNKS], mp_r.at[CHUNKS], other)
    trade.start()
    trades.append(trade)
    trade.wait_recv()
    n, i = layer_norm(nmine[...].astype(F32) + ntheirs[...].astype(F32))
    node_dout = norm_back(n, i, ncot_ref[...].astype(F32)).astype(BF)
    node_dpre = (nt(node_dout, nw2_ref[...]) * node_slope).astype(BF)
    gmine[...] = nt(node_dpre, nw1_ref[width : 2 * width]).astype(BF)
    trade = remote(gmine, gtheirs, mp_s.at[CHUNKS + 1], mp_r.at[CHUNKS + 1], other)
    trade.start()
    trades.append(trade)

    x = lax.rem(me, 2)
    z = lax.div(me, 2)
    near = z + 1 - 2 * lax.rem(z, 2)
    far = lax.rem(z + 2, 4)
    both = lax.rem(near + 2, 4)

    def spot(flips):
        along = {"": z, "0": near, "1": far, "01": both}
        return (1 - x if "x" in flips else x), along["".join(sorted(set(flips) - {"x"}))]

    def device(flips):
        across, along = spot(flips)
        return {"dom": along * 2 + across}

    routes = ("x01", "0x1", "x01", "0x1")

    def owners(which):
        first, second, third = routes[which]
        return first, second, third, (second + third, second, third, "")

    def first_hop(which, grad):
        buf, land = rs_refs[which][:2]
        size = grad.shape[0] // count
        for j in range(count):
            buf[j % 2, j // 2] = grad[j * size : (j + 1) * size].astype(BF)
        first, _, _, slices = owners(which)
        copies = []
        for k in range(4):
            copy = remote(
                buf.at[spot(first + slices[k])], land.at[k],
                rs_s.at[which, k], rs_r.at[which, k], device(first),
            )
            copy.start()
            copies.append(copy)
        sums[which] = copies

    def next_hop(which, k):
        copies = sums[which]
        buf, land, summed, land2 = rs_refs[which]
        _, second, third, slices = owners(which)
        copies[k].wait_recv()
        total = buf[spot(slices[k])].astype(F32) + land[k].astype(F32)
        if k == 2:
            copies[4].wait_recv()
            total = total + land2[0].astype(F32)
        summed[k] = total.astype(BF)
        copy = remote(
            summed.at[k], land2.at[k], rs_s.at[which, 4 + k], rs_r.at[which, 4 + k],
            device(second if k < 2 else third),
        )
        copy.start()
        copies.append(copy)

    def finish(which, out):
        copies = sums[which]
        buf, land, summed, land2 = rs_refs[which]
        copies[3].wait_recv()
        copies[5].wait_recv()
        total = buf[x, z].astype(F32) + land[3].astype(F32) + land2[1].astype(F32)
        copies[6].wait_recv()
        out[...] = total + land2[2].astype(F32)

    sums = {}
    node_w2_grad = tn(node_dout, node_act)
    if scatter:
        first_hop(1, node_w2_grad)
    node_w1_grad = jnp.concatenate([tn(node, node_dpre), tn(gathered, node_dpre)], axis=0)
    if scatter:
        first_hop(0, node_w1_grad)
    else:
        nw1_out[...] = node_w1_grad
        nw2_out[...] = node_w2_grad
    node_own = nt(node_dpre, nw1_ref[0:width])

    trade.wait_recv()
    gathered_grad = (gmine[...].astype(F32) + gtheirs[...].astype(F32)).astype(BF)
    for c in range(CHUNKS):
        r = pl.ds(c * rows, rows)
        upstream = live[r] * ecot_ref[r].astype(F32) + nn(
            pick_t[r, codes : codes + nodes], gathered_grad
        )
        d = norm_back(normed[r], inverse[r], upstream).astype(BF)
        dout[r] = d
        dpre[r] = (nt(d, w2_ref[...]) * slope[r]).astype(BF)
        if scatter and c > 0:
            next_hop(1, c - 1)
            next_hop(0, c - 1)
    edge_w2_grad = tn(dout[...], act[...])
    if scatter:
        first_hop(3, edge_w2_grad)
    merged = nn(pick[...], dpre[...]).astype(BF)
    by_code = merged[0:codes]
    by_node = merged[codes : codes + nodes]
    per_code = nt(by_code, w1_ref[width : 2 * width])
    back_out[...] = per_code[nodes:codes]
    backs = []
    for k in range(neigh):
        block = pl.ds(k * slots, slots)
        copy = remote(
            back_out.at[block], back_in.at[block], back_s.at[k], back_r.at[k],
            at(-offset_of(k, half)),
        )
        copy.start()
        backs.append(copy)
    edge_w1_grad = jnp.concatenate(
        [tn(edge_ref[...], dpre[...]), tn(sources[...], by_code), tn(node, by_node)], axis=0
    )
    if scatter:
        first_hop(2, edge_w1_grad)
        next_hop(1, 2)
        next_hop(0, 2)
    else:
        ew1_out[...] = edge_w1_grad
        ew2_out[...] = edge_w2_grad

    edge_trades = []
    for c in range(CHUNKS):
        r = pl.ds(c * rows, rows)
        dmine[r] = nt(dpre[r], w1_ref[0:width]).astype(BF)
        s = CHUNKS + 2 + c
        copy = remote(dmine.at[r], dtheirs.at[r], mp_s.at[s], mp_r.at[s], other)
        copy.start()
        edge_trades.append(copy)
    node_own = node_own + per_code[0:nodes] + nt(by_node, w1_ref[2 * width : 3 * width])
    if scatter:
        next_hop(3, 0)
        next_hop(2, 0)
    for c in range(CHUNKS):
        r = pl.ds(c * rows, rows)
        edge_trades[c].wait_recv()
        total = dmine[r].astype(F32) + dtheirs[r].astype(F32)
        egrad_ref[r] = (live[r] * (ecot_ref[r].astype(F32) + total)).astype(BF)
    stores = [load(12, egrad_ref, egrad_hbm)]
    if scatter:
        next_hop(3, 1)
        next_hop(2, 1)
    for copy in backs:
        copy.wait_recv()
    fmine[...] = node_own + nn(lists, back_in[...].astype(BF))
    last = 2 * CHUNKS + 2
    final = remote(fmine, ftheirs, mp_s.at[last], mp_r.at[last], other)
    final.start()
    if scatter:
        next_hop(3, 2)
        next_hop(2, 2)
        finish(1, nw2_out)
        finish(0, nw1_out)
    stores.append(load(15, nw1_out, nw1_grad_hbm))
    stores.append(load(16, nw2_out, nw2_grad_hbm))
    final.wait_recv()
    ngrad_ref[...] = (ncot_ref[...].astype(F32) + fmine[...] + ftheirs[...]).astype(BF)
    stores.append(load(11, ngrad_ref, ngrad_hbm))
    if scatter:
        finish(3, ew2_out)
        finish(2, ew1_out)
    stores.append(load(13, ew1_out, ew1_hbm))
    stores.append(load(14, ew2_out, ew2_hbm))
    if scatter:
        for copy in sums[0] + sums[1] + sums[2] + sums[3]:
            copy.wait_send()
    for copy in halo + trades + backs + edge_trades + [final]:
        copy.wait_send()
    for copy in stores:
        copy.wait()


def write_kernel(*refs):
    ins, outs, held, sems = refs[:6], refs[6:12], refs[12:18], refs[18]
    order = (1, 2, 4, 0, 3, 5)
    copies = {}
    for index in order:
        copies[index] = pltpu.make_async_copy(ins[index], held[index], sems.at[0, index])
        copies[index].start()
    stores = []
    for index in order:
        copies[index].wait()
        store = pltpu.make_async_copy(held[index], outs[index], sems.at[1, index])
        store.start()
        stores.append(store)
    for store in stores:
        store.wait()


def write_out(*results):
    return pl.pallas_call(
        write_kernel,
        out_shape=[jax.ShapeDtypeStruct(v.shape, v.dtype) for v in results],
        in_specs=[pl.BlockSpec(memory_space=pltpu.HBM)] * 6,
        out_specs=[pl.BlockSpec(memory_space=pltpu.HBM)] * 6,
        scratch_shapes=[pltpu.VMEM(v.shape, v.dtype) for v in results]
        + [pltpu.SemaphoreType.DMA((2, 6))],
        compiler_params=pltpu.CompilerParams(vmem_limit_bytes=VMEM_LIMIT),
    )(*results)


def local(
    count,
    node_latent,
    edge_latent,
    node_cot,
    edge_cot,
    edge_w1,
    edge_w2,
    node_w1,
    node_w2,
    send_rows,
    edge_sender,
    edge_receiver,
    edge_count,
):
    nodes, width = node_latent.shape
    edges = edge_latent.shape[0]
    hidden = edge_w1.shape[1]
    neigh, slots = send_rows.shape[1:]
    listed = neigh * slots
    codes = nodes + listed
    total = -(-(codes + nodes) // 128) * 128
    w1_rows, nw1_rows = edge_w1.shape[0], node_w1.shape[0]
    scatter = (
        count == 8
        and w1_rows % (16 * count) == 0
        and nw1_rows % (16 * count) == 0
        and width % (16 * count) == 0
    )
    parts = count if scatter else 1
    sizes = [r // parts if scatter else 16 for r in (nw1_rows, width, w1_rows, width)]
    vmem = pltpu.VMEM
    dma = pltpu.SemaphoreType.DMA
    scratch = [
        vmem((nodes, width), BF),
        vmem((edges, width), BF),
        vmem((nodes, width), BF),
        vmem((edges, width), BF),
        vmem(edge_w1.shape, BF),
        vmem(edge_w2.shape, BF),
        vmem(node_w1.shape, BF),
        vmem(node_w2.shape, BF),
        vmem((neigh, 1, slots), jnp.int32),
        vmem((edges,), jnp.int32),
        vmem((edges,), jnp.int32),
        vmem((nodes, listed), F32),
        vmem((total, edges), BF),
        vmem((edges, total), BF),
        vmem((edges, 1), F32),
        vmem((listed, width), F32),
        vmem((listed, width), F32),
        vmem((codes, width), BF),
        vmem((total, hidden), BF),
        vmem((edges, hidden), F32),
        vmem((edges, hidden), BF),
        vmem((edges, hidden), F32),
        vmem((edges, width), BF),
        vmem((edges, width), BF),
        vmem((edges, width), F32),
        vmem((edges, 1), F32),
        vmem((edges, width), BF),
        vmem((nodes, width), BF),
        vmem((nodes, width), BF),
        vmem((nodes, width), BF),
        vmem((nodes, width), BF),
        vmem((edges, width), BF),
        vmem((edges, hidden), BF),
        vmem((edges, width), BF),
        vmem((edges, width), BF),
        vmem((listed, width), F32),
        vmem((listed, width), F32),
        vmem((nodes, width), F32),
        vmem((nodes, width), F32),
        [
            (
                vmem((2, 4, size, hidden), BF),
                vmem((4, size, hidden), BF),
                vmem((3, size, hidden), BF),
                vmem((3, size, hidden), BF),
            )
            for size in sizes
        ],
        dma((neigh,)),
        dma((neigh,)),
        dma((neigh,)),
        dma((neigh,)),
        dma((2 * CHUNKS + 3,)),
        dma((2 * CHUNKS + 3,)),
        dma((4, 7)),
        dma((4, 7)),
        dma((17,)),
    ]
    shape = jax.ShapeDtypeStruct
    shapes = (
        shape((nodes, width), BF),
        shape((edges, width), BF),
        shape((w1_rows // parts, hidden), F32),
        shape((width // parts, hidden), F32),
        shape((nw1_rows // parts, hidden), F32),
        shape((width // parts, hidden), F32),
    )
    node_grad, edge_grad, ew1, ew2, nw1, nw2 = pl.pallas_call(
        functools.partial(kernel, (count, neigh, slots, scatter)),
        out_shape=shapes,
        in_specs=[pl.BlockSpec(memory_space=pltpu.HBM)] * 11
        + [pl.BlockSpec(memory_space=pltpu.SMEM)],
        out_specs=[pl.BlockSpec(memory_space=pltpu.HBM)] * 6,
        scratch_shapes=[vmem(v.shape, v.dtype) for v in shapes] + scratch,
        compiler_params=pltpu.CompilerParams(
            collective_id=0, has_side_effects=True, vmem_limit_bytes=VMEM_LIMIT
        ),
    )(
        node_latent, edge_latent, node_cot, edge_cot, edge_w1, edge_w2, node_w1, node_w2,
        jnp.transpose(send_rows, (1, 0, 2)), edge_sender, edge_receiver, edge_count,
    )
    if scatter:
        node_grad, edge_grad, ew1, ew2, nw1, nw2 = write_out(
            node_grad, edge_grad, ew1, ew2, nw1, nw2
        )
        return node_grad, edge_grad, ew1, ew2.T, nw1, nw2.T
    ew2, nw2 = ew2.T, nw2.T
    ew1, nw1 = (lax.psum_scatter(g, "dom", scatter_dimension=0, tiled=True) for g in (ew1, nw1))
    ew2, nw2 = (lax.psum_scatter(g, "dom", scatter_dimension=1, tiled=True) for g in (ew2, nw2))
    return node_grad, edge_grad, ew1, ew2, nw1, nw2


def solution(mesh):
    placed = (
        P(("groups", "dom"), None),
        P(("groups", "dom"), None),
        P(("groups", "dom"), None),
        P(("groups", "dom"), None),
        P(None, "mp"),
        P("mp", None),
        P(None, "mp"),
        P("mp", None),
        P("dom", None, None),
        P("dom"),
        P("dom"),
        P("dom"),
    )
    return jax.shard_map(
        functools.partial(local, mesh.shape["dom"]),
        mesh=mesh,
        in_specs=placed,
        out_specs=(
            P(("groups", "dom"), None),
            P(("groups", "dom"), None),
            P(("groups", "dom"), "mp"),
            P(("groups", "mp"), "dom"),
            P(("groups", "dom"), "mp"),
            P(("groups", "mp"), "dom"),
        ),
        check_vma=False,
    )
```
